32 devices in a mesh: head: 2 (over x), blk: 16 (over z, y, core).
Axes of the slice: x: 2, y: 2, z: 4, core: 2. Of those that a mesh axis runs over, the one named last changes fastest.
Arguments:
- queries: bfloat16 [2, 6144, 5120], P('head', 'blk'), may hold values from -8 to 8
- keys: bfloat16 [2, 6144, 5120], P('head', 'blk'), may hold values from -8 to 8
- values: bfloat16 [2, 6144, 5120], P('head', 'blk'), may hold values from -6 to 6
- q_gain: float32 [5120], replicated, may hold values from 0.1 to 1.9
- k_gain: float32 [5120], replicated, may hold values from 0.1 to 1.9
- slopes: float32 [40], P('head'), may hold values from 0.25 to 4
- out_weight: bfloat16 [5120, 5120], P('head', 'blk'), may hold values from -1 to 1
- kv_tiles: int32 [32, 4], replicated, may hold values from 0 to 31, as said below
- tile_frame: int32 [32], replicated, may hold values from 0 to 3, never falling along the last dimension, each value on 1 to 16 neighbouring positions
Outputs:
- mixed: bfloat16 [2, 6144, 5120], P('head', 'blk')
The draws below stay inside these ranges and needn't reach their ends.
Inputs may be any that keep to these rules, and one draw needn't show every extreme that they name: kv_tiles[t, 0] = t; the other entries of row t are distinct tiles other than t, each within 3 tiles of t. `tile_frame`: never falls from one tile to the next.
All inputs are finite; a program needn't handle non-finite values.
Results may differ from the reference program's by a relative error of at most 0.013.
Values may be sent and summed in bfloat16 or wider, within the bound.
A program may use at most 256 MiB of HBM per device.

```python
import math
import jax
import jax.numpy as jnp
import numpy as np
from jax import lax

D = 5120
HEADS = 40
HDIM = 128
TILE = 384
HD = 5120
GROUPS = 2
T_DEV = 384
NTILES = 32
TOKENS = 12288
REACH = 3
WIN = 4
FRAMES = 4
N_HEAD = 2
N_BLK = 16


def paired_rows(key):
    rows = TOKENS // GROUPS
    first = jax.random.fold_in(key, 101)
    second = jax.random.fold_in(key, 102)
    third = jax.random.fold_in(key, 103)
    raw = jax.random.normal(first, (2, GROUPS, rows, HD), jnp.float32)
    column_scale = jnp.exp(jax.random.uniform(second, (2, 1, 1, HD), jnp.float32, math.log(0.3), math.log(3.0)))
    row_scale = jnp.exp(jax.random.uniform(third, (2, GROUPS, rows, 1), jnp.float32, math.log(0.3), math.log(3.0)))
    both = raw * column_scale * row_scale
    query_rows = both[0]
    key_rows = both[1]
    return (jnp.clip(query_rows, -8.0, 8.0), jnp.clip(key_rows, -8.0, 8.0))


def draw_queries(key, part):
    return paired_rows(key)[0].astype(jnp.bfloat16)


def draw_keys(key, part):
    return paired_rows(key)[1].astype(jnp.bfloat16)


def draw_kv_tiles(key, part):
    span = 2 * REACH + 1
    offsets = jnp.arange(span) - REACH
    tiles = jnp.arange(NTILES)
    candidates = tiles[:, None] + offsets[None, :]
    usable = (candidates >= 0) & (candidates < NTILES) & (offsets[None, :] != 0)
    scores = jax.random.randint(jax.random.fold_in(key, 7), (NTILES, span), 0, 1 << 20)
    scores = scores * span + jnp.arange(span)[None, :]
    scores = jnp.where(usable, scores, -1 - jnp.arange(span)[None, :])
    picked = lax.top_k(scores, WIN - 1)[1]
    chosen = jnp.take_along_axis(candidates, picked, axis=1)
    return jnp.concatenate([tiles[:, None], chosen], axis=1).astype(jnp.int32)


def levels(key, shape, split, low, largest):
    factor_of = 1.0
    for axis_at, blocks in split:
        steps = jax.random.uniform(jax.random.fold_in(jax.random.fold_in(key, 6), axis_at), (blocks,), jnp.float32, low / len(split), largest / len(split))
        factor_of = factor_of * jnp.repeat(jnp.exp(steps), shape[axis_at] // blocks).reshape((-1,) + (1,) * (len(shape) - 1 - axis_at))
    return factor_of


def length_profile(amount, total, bound, skew):
    portions = [(1 << 20) // math.isqrt(rank ** skew) + 1 for rank in range(2, amount + 1)]
    surplus, holding = total - bound - (amount - 1), [1] * (amount - 1)
    while surplus > 0:
        movable = [i for i in range(amount - 1) if holding[i] < bound]
        whole, left = sum([portions[i] for i in movable]), surplus
        for i in movable:
            extra = min(bound - holding[i], max(1, left * portions[i] // whole), surplus)
            holding[i] = holding[i] + extra
            surplus = surplus - extra
    return np.array([bound] + holding)


def ragged(rng, count, total, bound, slope):
    if count == 2:
        one = jax.random.randint(rng, (), max(1, total - bound), min(bound, total - 1) + 1)
        return jnp.stack([one, total - one])
    sizes = jnp.asarray(length_profile(count, total, bound, slope), jnp.int32)
    twos = (count - 1) // 2
    donor, sink = sizes[1:1 + 2 * twos:2], sizes[2:2 + 2 * twos:2]
    slack = jnp.minimum(donor - 1, bound - sink)
    moved = jax.random.randint(jax.random.fold_in(rng, 1), (twos,), 0, 1 << 20) % (slack + 1)
    sizes = sizes.at[1:1 + 2 * twos:2].set(donor - moved).at[2:2 + 2 * twos:2].set(sink + moved)
    return sizes[jax.random.permutation(jax.random.fold_in(rng, 2), count)]


def scatter_about(key, dims, deviation, bound, cuts=(), dtype=jnp.bfloat16):
    values = jax.random.normal(key, dims, jnp.float32) * deviation
    if len(cuts) > 0:
        values = levels(key, dims, cuts, -0.22, 0.18) * values
    return jnp.clip(values, min=-bound, max=bound).astype(dtype)


def setup_inputs(seed: int = 0) -> dict:
    arg_keys = jax.random.split(jax.random.key(seed), 10)
    queries = draw_queries(jax.random.fold_in(arg_keys[9], 71), 0)
    keys = draw_keys(jax.random.fold_in(arg_keys[9], 71), 0)
    values = scatter_about(arg_keys[2], (GROUPS, N_BLK * T_DEV, HD), 1.0, 6.0, ((0, 2), (1, 16)))
    q_gain = jnp.clip(1.0 + 0.18 * jax.random.normal(arg_keys[3], (HD,), jnp.float32), 0.1, 1.9)
    k_gain = jnp.clip(1.0 + 0.18 * jax.random.normal(arg_keys[4], (HD,), jnp.float32), 0.1, 1.9)
    slopes = jnp.clip(jnp.exp(math.log(4.0) - 2.7725887 * jax.random.uniform(arg_keys[5], (HEADS,), jnp.float32) ** levels(arg_keys[5], (HEADS,), ((0, 2),), -0.2, 0.2)), 0.25, 4.0)
    out_weight = scatter_about(arg_keys[6], (HD, D), (HDIM // 4) ** -0.5, 1.0, ((0, 2), (1, 16)))
    kv_tiles = draw_kv_tiles(jax.random.fold_in(arg_keys[9], 71), 0)
    tile_frame = jnp.searchsorted(jnp.cumsum(ragged(arg_keys[8], FRAMES, NTILES, 16, 2)), jnp.arange(NTILES), side="right").astype(jnp.int32)
    return {"queries": queries, "keys": keys, "values": values, "q_gain": q_gain, "k_gain": k_gain, "slopes": slopes, "out_weight": out_weight, "kv_tiles": kv_tiles, "tile_frame": tile_frame}


def rms_norm(rows, gain):
    floats = rows.astype(jnp.float32)
    factor = lax.rsqrt(lax.optimization_barrier(jnp.mean(floats * floats, axis=-1, keepdims=True)) + 1e-06)
    return (floats * factor * gain).astype(jnp.bfloat16)

def to_sequence(array):
    groups, rows, width = array.shape
    return array.reshape(groups, N_BLK, rows // N_BLK, width).transpose(1, 0, 2, 3).reshape(groups * rows, width)

def reference(queries, keys, values, q_gain, k_gain, slopes, out_weight, kv_tiles, tile_frame):
    query_tiles = to_sequence(rms_norm(queries, q_gain)).reshape(NTILES, TILE, HEADS, HDIM)
    key_tiles = to_sequence(rms_norm(keys, k_gain)).reshape(NTILES, TILE, HEADS, HDIM)
    value_tiles = to_sequence(values).reshape(NTILES, TILE, HEADS, HDIM)

    def one_tile(tile):
        listed = kv_tiles[tile]
        near_keys = key_tiles[listed].reshape(WIN * TILE, HEADS, HDIM).astype(jnp.float32)
        near_values = value_tiles[listed].reshape(WIN * TILE, HEADS, HDIM).astype(jnp.float32)
        score = jnp.einsum('qhd,khd->hqk', query_tiles[tile].astype(jnp.float32), near_keys) * HDIM ** (-0.5)
        frame_gap = jnp.abs(tile_frame[tile] - tile_frame[listed]).astype(jnp.float32)
        penalty = slopes[:, None] * frame_gap[None, :]
        score = (score.reshape(HEADS, TILE, WIN, TILE) - penalty[:, None, :, None]).reshape(HEADS, TILE, WIN * TILE)
        weight = jnp.exp(score - lax.optimization_barrier(jnp.max(score, axis=-1, keepdims=True)))
        total = lax.optimization_barrier(jnp.sum(weight, axis=-1))
        rounded = weight.astype(jnp.bfloat16).astype(jnp.float32)
        summed = jnp.einsum('hqk,khd->qhd', rounded, near_values)
        return (summed / jnp.transpose(total)[:, :, None]).astype(jnp.bfloat16)
    attended = lax.map(one_tile, jnp.arange(NTILES)).reshape(TOKENS, HD)
    group_width = HD // N_HEAD
    mixed = jnp.zeros((TOKENS, D), jnp.float32)
    for group in range(N_HEAD):
        columns = attended[:, group * group_width:(group + 1) * group_width]
        weight_rows = out_weight[group * group_width:(group + 1) * group_width]
        partial_value = jnp.dot(columns, weight_rows, preferred_element_type=jnp.float32).astype(jnp.bfloat16)
        partial_value = lax.optimization_barrier(partial_value)
        mixed = mixed + partial_value.astype(jnp.float32)
    mixed = mixed.astype(jnp.bfloat16)
    return mixed.reshape(N_BLK, GROUPS, T_DEV, D).transpose(1, 0, 2, 3).reshape(GROUPS, N_BLK * T_DEV, D)
```

```python
import math

import jax
import jax.numpy as jnp
from jax import lax
from jax.experimental import pallas as pl
from jax.experimental.pallas import tpu as pltpu
from jax.sharding import PartitionSpec as P

HDIM = 128
TILE = 384
REACH = 3
LOG2E = math.log2(math.e)
CHUNKS = 4


def shifted(value, axis, steps):
    count = lax.axis_size(axis)
    initial, last = (max(0, -steps), min(count, count - steps))
    return lax.ppermute(value, axis, [(source, source + steps) for source in range(initial, last)])


def rms_norm(rows, gain):
    floats = rows.astype(jnp.float32)
    factor = lax.rsqrt(jnp.mean(floats * floats, axis=-1, keepdims=True) + 1e-06)
    return (floats * factor * gain).astype(jnp.bfloat16)


def attend_kernel(tiles, wins, parts, index_ref, penalty_ref, *refs):
    q_ref = refs[0]
    key_refs = refs[1 : 1 + parts]
    value_refs = refs[1 + parts : 1 + 2 * parts]
    out_ref, key_window, value_window = refs[1 + 2 * parts :]
    head = pl.program_id(0)
    for window, blocks in ((key_window, key_refs), (value_window, value_refs)):
        at = 0
        for block in blocks:
            for tile in range(block.shape[0] // TILE):
                window[at] = block[tile * TILE : (tile + 1) * TILE, :]
                at += 1
    for tile in range(tiles):
        query = q_ref[tile * TILE : (tile + 1) * TILE, :]
        scores = []
        largest = None
        for win in range(wins):
            near = key_window[index_ref[tile * wins + win]]
            score = lax.dot_general(
                query, near, (((1,), (1,)), ((), ())), preferred_element_type=jnp.float32
            )
            penalty = penalty_ref[(head * tiles + tile) * wins + win]
            top = jnp.max(score, axis=-1, keepdims=True) - penalty
            largest = top if largest is None else jnp.maximum(largest, top)
            scores.append((score, penalty))
        total = jnp.zeros((TILE, 1), jnp.float32)
        summed = jnp.zeros((TILE, HDIM), jnp.float32)
        for win, (score, penalty) in enumerate(scores):
            weight = jnp.exp2(score - (largest + penalty))
            total += jnp.sum(weight, axis=-1, keepdims=True)
            summed += jnp.dot(
                weight.astype(jnp.bfloat16),
                value_window[index_ref[tile * wins + win]],
                preferred_element_type=jnp.float32,
            )
        out_ref[tile * TILE : (tile + 1) * TILE, :] = (summed / total).astype(out_ref.dtype)


def attend(query, key_parts, value_parts, index, penalty):
    rows, width = query.shape
    heads, tiles, wins = width // HDIM, rows // TILE, index.shape[0] * TILE // rows
    window = sum(part.shape[0] for part in key_parts) // TILE

    def column(array):
        return pl.BlockSpec((array.shape[0], HDIM), lambda h, *_: (0, h))

    def body(*refs):
        attend_kernel(tiles, wins, len(key_parts), *refs)

    operands = (query, *key_parts, *value_parts)
    return pl.pallas_call(
        body,
        grid_spec=pltpu.PrefetchScalarGridSpec(
            num_scalar_prefetch=2,
            grid=(heads,),
            in_specs=[column(array) for array in operands],
            out_specs=column(query),
            scratch_shapes=[pltpu.VMEM((window, TILE, HDIM), jnp.bfloat16)] * 2,
        ),
        out_shape=jax.ShapeDtypeStruct(query.shape, jnp.bfloat16),
        compiler_params=pltpu.CompilerParams(vmem_limit_bytes=48 * 1024 * 1024),
        cost_estimate=pl.CostEstimate(
            flops=4 * rows * wins * TILE * width,
            bytes_accessed=2 * sum(array.size for array in operands) + 2 * query.size,
            transcendentals=rows * wins * TILE * heads,
        ),
    )(index, penalty, *operands)


def halo(own, tiles):
    near = min(REACH, tiles)
    far = REACH - near
    last = own.shape[0]
    lower, upper = [], []
    if far:
        lower.append(shifted(own[last - far * TILE :], "blk", 2))
        upper.append(shifted(own[: far * TILE], "blk", -2))
    lower.append(shifted(own[last - near * TILE :], "blk", 1))
    upper.insert(0, shifted(own[: near * TILE], "blk", -1))
    return [*lower, own, *upper]


def shards(queries, keys, values, q_gain, k_gain, slopes, out_weight, kv_tiles, tile_frame):
    groups = lax.axis_size("head")
    position, group = lax.axis_index("blk"), lax.axis_index("head")

    def to_heads(rows):
        return lax.all_to_all(rows, "head", split_axis=1, concat_axis=0, tiled=True)

    full_columns = lax.all_gather(out_weight, "blk", axis=1, tiled=True)
    value_own = to_heads(values[0])
    key_own = to_heads(rms_norm(keys[0], k_gain))
    query_own = to_heads(rms_norm(queries[0], q_gain * (LOG2E * HDIM ** (-0.5))))
    tiles = query_own.shape[0] // TILE
    key_parts, value_parts = halo(key_own, tiles), halo(value_own, tiles)

    listed = lax.dynamic_slice_in_dim(kv_tiles, position * tiles, tiles, 0)
    own_frames = lax.dynamic_slice_in_dim(tile_frame, position * tiles, tiles, 0)
    gap = jnp.abs(own_frames[:, None] - jnp.take(tile_frame, listed, axis=0)).astype(jnp.float32)
    penalty = (slopes * LOG2E)[:, None] * gap.reshape(1, -1)
    index = (listed - (position * tiles - REACH)).reshape(-1)
    attended = attend(query_own, key_parts, value_parts, index, penalty.reshape(-1))

    rows = attended.shape[0] // groups
    width = full_columns.shape[1] // CHUNKS

    def partial(owner, chunk):
        return jnp.dot(
            lax.dynamic_slice_in_dim(attended, owner * rows, rows, 0),
            full_columns[:, chunk * width : (chunk + 1) * width],
            preferred_element_type=jnp.float32,
        ).astype(jnp.bfloat16)

    arrived = []
    for chunk in range(CHUNKS):
        arrived.append(
            [
                lax.ppermute(
                    partial(lax.rem(group + step, groups), chunk),
                    "head",
                    [(source, (source + step) % groups) for source in range(groups)],
                )
                for step in range(1, groups)
            ]
        )
    mixed = []
    for chunk in range(CHUNKS):
        floats = partial(group, chunk).astype(jnp.float32)
        for term in arrived[chunk]:
            floats = floats + term.astype(jnp.float32)
        mixed.append(floats.astype(jnp.bfloat16))
    return jnp.concatenate(mixed, axis=1)[None]


def solution(mesh):
    placed = (
        P("head", "blk", None),
        P("head", "blk", None),
        P("head", "blk", None),
        P(),
        P(),
        P("head"),
        P("head", "blk"),
        P(),
        P(),
    )
    return jax.shard_map(
        shards, mesh=mesh, in_specs=placed, out_specs=P("head", "blk", None), check_vma=False
    )
```

```python
import math

import jax
import jax.numpy as jnp
from jax import lax
from jax.experimental import pallas as pl
from jax.experimental.pallas import tpu as pltpu
from jax.sharding import PartitionSpec as P

HDIM = 128
TILE = 384
REACH = 3
LOG2E = math.log2(math.e)
CHUNKS = 4
TEAM = 8
STEP = 2


def shifted(value, axis, steps):
    count = lax.axis_size(axis)
    initial, last = (max(0, -steps), min(count, count - steps))
    return lax.ppermute(value, axis, [(source, source + steps) for source in range(initial, last)])


def rms_norm(rows, gain):
    floats = rows.astype(jnp.float32)
    factor = lax.rsqrt(jnp.mean(floats * floats, axis=-1, keepdims=True) + 1e-06)
    return (floats * factor * gain).astype(jnp.bfloat16)


def attend_kernel(tiles, wins, parts, index_ref, penalty_ref, *refs):
    q_ref = refs[0]
    key_refs = refs[1 : 1 + parts]
    value_refs = refs[1 + parts : 1 + 2 * parts]
    out_ref, key_window, value_window = refs[1 + 2 * parts :]
    head = pl.program_id(0)
    first = pl.program_id(1) * STEP

    @pl.when(first == 0)
    def _():
        for window, blocks in ((key_window, key_refs), (value_window, value_refs)):
            at = 0
            for block in blocks:
                for tile in range(block.shape[0] // TILE):
                    window[at] = block[tile * TILE : (tile + 1) * TILE, :]
                    at += 1

    for step in range(STEP):
        tile = first + step
        query = q_ref[step * TILE : (step + 1) * TILE, :]
        scores = []
        largest = None
        for win in range(wins):
            near = key_window[index_ref[tile * wins + win]]
            score = lax.dot_general(
                query, near, (((1,), (1,)), ((), ())), preferred_element_type=jnp.float32
            )
            penalty = penalty_ref[(head * tiles + tile) * wins + win]
            top = jnp.max(score, axis=-1, keepdims=True) - penalty
            largest = top if largest is None else jnp.maximum(largest, top)
            scores.append((score, penalty))
        total = jnp.zeros((TILE, 1), jnp.float32)
        summed = jnp.zeros((TILE, HDIM), jnp.float32)
        for win, (score, penalty) in enumerate(scores):
            weight = jnp.exp2(score - (largest + penalty))
            total += jnp.sum(weight, axis=-1, keepdims=True)
            summed += jnp.dot(
                weight.astype(jnp.bfloat16),
                value_window[index_ref[tile * wins + win]],
                preferred_element_type=jnp.float32,
            )
        out_ref[step * TILE : (step + 1) * TILE, :] = (summed / total).astype(out_ref.dtype)


def attend(query, key_parts, value_parts, index, penalty):
    rows, width = query.shape
    heads, tiles, wins = width // HDIM, rows // TILE, index.shape[0] * TILE // rows
    window = sum(part.shape[0] for part in key_parts) // TILE

    def column(array):
        return pl.BlockSpec((array.shape[0], HDIM), lambda h, t, *_: (0, h))

    stepped = pl.BlockSpec((STEP * TILE, HDIM), lambda h, t, *_: (t, h))

    def body(*refs):
        attend_kernel(tiles, wins, len(key_parts), *refs)

    operands = (query, *key_parts, *value_parts)
    return pl.pallas_call(
        body,
        grid_spec=pltpu.PrefetchScalarGridSpec(
            num_scalar_prefetch=2,
            grid=(heads, tiles // STEP),
            in_specs=[stepped, *(column(array) for array in operands[1:])],
            out_specs=stepped,
            scratch_shapes=[pltpu.VMEM((window, TILE, HDIM), jnp.bfloat16)] * 2,
        ),
        out_shape=jax.ShapeDtypeStruct(query.shape, jnp.bfloat16),
        compiler_params=pltpu.CompilerParams(vmem_limit_bytes=48 * 1024 * 1024),
        cost_estimate=pl.CostEstimate(
            flops=4 * rows * wins * TILE * width,
            bytes_accessed=2 * sum(array.size for array in operands) + 2 * query.size,
            transcendentals=rows * wins * TILE * heads,
        ),
    )(index, penalty, *operands)


def halo(own, hop):
    reach = REACH * TILE
    lower = shifted(own[own.shape[0] - reach :], "blk", hop)
    upper = shifted(own[:reach], "blk", -hop)
    return [lower, own, upper]


def shards(queries, keys, values, q_gain, k_gain, slopes, out_weight, kv_tiles, tile_frame):
    groups, blocks = lax.axis_size("head"), lax.axis_size("blk")
    position, group = lax.axis_index("blk"), lax.axis_index("head")
    hop = TEAM // groups
    member = lax.rem(position, hop)
    teams = [
        [head * blocks + first + inner for inner in range(hop) for head in range(groups)]
        for first in range(0, blocks, hop)
    ]
    lines = [list(range(first, first + hop)) for first in range(0, blocks, hop)]
    length, features = values.shape[1:]
    narrow = features // TEAM

    def to_heads(rows):
        parts = rows.reshape(length, groups, hop, narrow).transpose(2, 1, 0, 3)
        parts = lax.all_to_all(
            parts.reshape(TEAM, length, narrow),
            ("head", "blk"),
            split_axis=0,
            concat_axis=0,
            axis_index_groups=teams,
            tiled=True,
        )
        return parts.reshape(TEAM * length, narrow)

    full_columns = lax.all_gather(out_weight, "blk", axis=1, tiled=True)
    value_own = to_heads(values[0])
    key_own = to_heads(rms_norm(keys[0], k_gain))
    query_own = to_heads(rms_norm(queries[0], q_gain * (LOG2E * HDIM ** (-0.5))))
    tiles = query_own.shape[0] // TILE
    key_parts, value_parts = halo(key_own, hop), halo(value_own, hop)

    start = position // hop * tiles
    listed = lax.dynamic_slice_in_dim(kv_tiles, start, tiles, 0)
    own_frames = lax.dynamic_slice_in_dim(tile_frame, start, tiles, 0)
    gap = jnp.abs(own_frames[:, None] - jnp.take(tile_frame, listed, axis=0)).astype(jnp.float32)
    heads = narrow // HDIM
    own_slopes = lax.dynamic_slice_in_dim(slopes, member * heads, heads, 0)
    penalty = (own_slopes * LOG2E)[:, None] * gap.reshape(1, -1)
    index = (listed - (start - REACH)).reshape(-1)
    attended = attend(query_own, key_parts, value_parts, index, penalty.reshape(-1))
    attended = lax.all_to_all(
        attended.reshape(hop, groups * length, narrow),
        "blk",
        split_axis=0,
        concat_axis=0,
        axis_index_groups=lines,
        tiled=True,
    )
    attended = attended.transpose(1, 0, 2).reshape(groups * length, hop * narrow)

    rows = attended.shape[0] // groups
    width = full_columns.shape[1] // CHUNKS

    def partial(owner, chunk):
        return jnp.dot(
            lax.dynamic_slice_in_dim(attended, owner * rows, rows, 0),
            full_columns[:, chunk * width : (chunk + 1) * width],
            preferred_element_type=jnp.float32,
        ).astype(jnp.bfloat16)

    arrived = []
    for chunk in range(CHUNKS):
        arrived.append(
            [
                lax.ppermute(
                    partial(lax.rem(group + step, groups), chunk),
                    "head",
                    [(source, (source + step) % groups) for source in range(groups)],
                )
                for step in range(1, groups)
            ]
        )
    mixed = []
    for chunk in range(CHUNKS):
        floats = partial(group, chunk).astype(jnp.float32)
        for term in arrived[chunk]:
            floats = floats + term.astype(jnp.float32)
        mixed.append(floats.astype(jnp.bfloat16))
    return jnp.concatenate(mixed, axis=1)[None]


def solution(mesh):
    placed = (
        P("head", "blk", None),
        P("head", "blk", None),
        P("head", "blk", None),
        P(),
        P(),
        P("head"),
        P("head", "blk"),
        P(),
        P(),
    )
    return jax.shard_map(
        shards, mesh=mesh, in_specs=placed, out_specs=P("head", "blk", None), check_vma=False
    )
```

```python
import math

import jax
import jax.numpy as jnp
from jax import lax
from jax.experimental import pallas as pl
from jax.experimental.pallas import tpu as pltpu
from jax.sharding import PartitionSpec as P

HDIM = 128
TILE = 384
REACH = 3
LOG2E = math.log2(math.e)
CHUNKS = 4
TEAM = 8
STEP = 2


def shifted(value, axis, steps):
    count = lax.axis_size(axis)
    initial, last = (max(0, -steps), min(count, count - steps))
    return lax.ppermute(value, axis, [(source, source + steps) for source in range(initial, last)])


def rms_norm(rows, gain):
    floats = rows.astype(jnp.float32)
    factor = lax.rsqrt(jnp.mean(floats * floats, axis=-1, keepdims=True) + 1e-06)
    return (floats * factor * gain).astype(jnp.bfloat16)


def attend_kernel(tiles, wins, parts, index_ref, penalty_ref, *refs):
    q_ref = refs[0]
    key_refs = refs[1 : 1 + parts]
    value_refs = refs[1 + parts : 1 + 2 * parts]
    out_ref, key_window, value_window = refs[1 + 2 * parts :]
    head = pl.program_id(0)
    first = pl.program_id(1) * STEP

    @pl.when(first == 0)
    def _():
        for window, blocks in ((key_window, key_refs), (value_window, value_refs)):
            at = 0
            for block in blocks:
                for tile in range(block.shape[0] // TILE):
                    window[at] = block[tile * TILE : (tile + 1) * TILE, :]
                    at += 1

    for step in range(STEP):
        tile = first + step
        query = q_ref[step * TILE : (step + 1) * TILE, :]
        scores = []
        largest = None
        for win in range(wins):
            near = key_window[index_ref[tile * wins + win]]
            score = lax.dot_general(
                query, near, (((1,), (1,)), ((), ())), preferred_element_type=jnp.float32
            )
            penalty = penalty_ref[(head * tiles + tile) * wins + win]
            top = jnp.max(score, axis=-1, keepdims=True) - penalty
            largest = top if largest is None else jnp.maximum(largest, top)
            scores.append((score, penalty))
        total = jnp.zeros((TILE, 1), jnp.float32)
        summed = jnp.zeros((TILE, HDIM), jnp.float32)
        for win, (score, penalty) in enumerate(scores):
            weight = jnp.exp2(score - (largest + penalty))
            total += jnp.sum(weight, axis=-1, keepdims=True)
            summed += jnp.dot(
                weight.astype(jnp.bfloat16),
                value_window[index_ref[tile * wins + win]],
                preferred_element_type=jnp.float32,
            )
        out_ref[step * TILE : (step + 1) * TILE, :] = (summed / total).astype(out_ref.dtype)


def attend(query, key_parts, value_parts, index, penalty):
    rows, width = query.shape
    heads, tiles, wins = width // HDIM, rows // TILE, index.shape[0] * TILE // rows
    window = sum(part.shape[0] for part in key_parts) // TILE

    def column(array):
        return pl.BlockSpec((array.shape[0], HDIM), lambda h, t, *_: (0, h))

    stepped = pl.BlockSpec((STEP * TILE, HDIM), lambda h, t, *_: (t, h))

    def body(*refs):
        attend_kernel(tiles, wins, len(key_parts), *refs)

    operands = (query, *key_parts, *value_parts)
    return pl.pallas_call(
        body,
        grid_spec=pltpu.PrefetchScalarGridSpec(
            num_scalar_prefetch=2,
            grid=(heads, tiles // STEP),
            in_specs=[stepped, *(column(array) for array in operands[1:])],
            out_specs=stepped,
            scratch_shapes=[pltpu.VMEM((window, TILE, HDIM), jnp.bfloat16)] * 2,
        ),
        out_shape=jax.ShapeDtypeStruct(query.shape, jnp.bfloat16),
        compiler_params=pltpu.CompilerParams(vmem_limit_bytes=48 * 1024 * 1024),
        cost_estimate=pl.CostEstimate(
            flops=4 * rows * wins * TILE * width,
            bytes_accessed=2 * sum(array.size for array in operands) + 2 * query.size,
            transcendentals=rows * wins * TILE * heads,
        ),
    )(index, penalty, *operands)


def halo(own, hop):
    reach = REACH * TILE
    lower = shifted(own[own.shape[0] - reach :], "blk", hop)
    upper = shifted(own[:reach], "blk", -hop)
    return [lower, own, upper]


def shards(queries, keys, values, q_gain, k_gain, slopes, out_weight, kv_tiles, tile_frame):
    groups, blocks = lax.axis_size("head"), lax.axis_size("blk")
    position, group = lax.axis_index("blk"), lax.axis_index("head")
    hop = TEAM // groups
    member = lax.rem(position, hop)
    teams = [
        [head * blocks + first + inner for inner in range(hop) for head in range(groups)]
        for first in range(0, blocks, hop)
    ]
    lines = [list(range(first, first + hop)) for first in range(0, blocks, hop)]
    length, features = values.shape[1:]
    narrow = features // TEAM

    def to_heads(rows):
        parts = rows.reshape(length, groups, hop, narrow).transpose(2, 1, 0, 3)
        parts = lax.all_to_all(
            parts.reshape(TEAM, length, narrow),
            ("head", "blk"),
            split_axis=0,
            concat_axis=0,
            axis_index_groups=teams,
            tiled=True,
        )
        return parts.reshape(TEAM * length, narrow)

    full_columns = lax.all_gather(out_weight, "blk", axis=1, tiled=True)
    value_own = to_heads(values[0])
    key_own = to_heads(rms_norm(keys[0], k_gain))
    value_parts = halo(value_own, hop)
    query_normed = rms_norm(queries[0], q_gain * (LOG2E * HDIM ** (-0.5)))
    query_normed, value_parts[0], value_parts[2] = lax.optimization_barrier(
        (query_normed, value_parts[0], value_parts[2])
    )
    query_own = to_heads(query_normed)
    tiles = query_own.shape[0] // TILE
    key_parts = halo(key_own, hop)

    start = position // hop * tiles
    listed = lax.dynamic_slice_in_dim(kv_tiles, start, tiles, 0)
    own_frames = lax.dynamic_slice_in_dim(tile_frame, start, tiles, 0)
    gap = jnp.abs(own_frames[:, None] - jnp.take(tile_frame, listed, axis=0)).astype(jnp.float32)
    heads = narrow // HDIM
    own_slopes = lax.dynamic_slice_in_dim(slopes, member * heads, heads, 0)
    penalty = (own_slopes * LOG2E)[:, None] * gap.reshape(1, -1)
    index = (listed - (start - REACH)).reshape(-1)
    attended = attend(query_own, key_parts, value_parts, index, penalty.reshape(-1))
    attended = lax.all_to_all(
        attended.reshape(hop, groups * length, narrow),
        "blk",
        split_axis=0,
        concat_axis=0,
        axis_index_groups=lines,
        tiled=True,
    )
    attended = attended.transpose(1, 0, 2).reshape(groups * length, hop * narrow)

    rows = attended.shape[0] // groups
    width = full_columns.shape[1] // CHUNKS

    def partial(owner, chunk):
        return jnp.dot(
            lax.dynamic_slice_in_dim(attended, owner * rows, rows, 0),
            full_columns[:, chunk * width : (chunk + 1) * width],
            preferred_element_type=jnp.float32,
        ).astype(jnp.bfloat16)

    arrived = []
    for chunk in range(CHUNKS):
        arrived.append(
            [
                lax.ppermute(
                    partial(lax.rem(group + step, groups), chunk),
                    "head",
                    [(source, (source + step) % groups) for source in range(groups)],
                )
                for step in range(1, groups)
            ]
        )
    mixed = []
    for chunk in range(CHUNKS):
        floats = partial(group, chunk).astype(jnp.float32)
        for term in arrived[chunk]:
            floats = floats + term.astype(jnp.float32)
        mixed.append(floats.astype(jnp.bfloat16))
    return jnp.concatenate(mixed, axis=1)[None]


def solution(mesh):
    placed = (
        P("head", "blk", None),
        P("head", "blk", None),
        P("head", "blk", None),
        P(),
        P(),
        P("head"),
        P("head", "blk"),
        P(),
        P(),
    )
    return jax.shard_map(
        shards, mesh=mesh, in_specs=placed, out_specs=P("head", "blk", None), check_vma=False
    )
```
